32 devices in a mesh: lev: 4 (over y, core), tile: 8 (over z, x).
Axes of the slice: x: 2, y: 2, z: 4, core: 2. Of those that a mesh axis runs over, the one named last changes fastest.
Arguments:
- fields: float32 [64, 5, 64, 512], P('lev', None, 'tile'), may hold values from -4 to 4
- land_use: int32 [64, 512], P('tile'), may hold values from 0 to 7
- column_ops: float32 [5, 8, 64, 64], replicated, may hold values from -1 to 1, as said below
Outputs:
- fields_new: float32 [64, 5, 64, 512], P('lev', None, 'tile')
The draws below stay inside these ranges and needn't reach their ends.
Inputs may be any that keep to these rules, and one draw needn't show every extreme that they name: `column_ops`: each matrix has independent entries.
All inputs are finite; a program needn't handle non-finite values.
Results may differ from the reference program's by a relative error of at most 0.0001.
Values sent between devices are 32-bit elements; how exact they have to be, the bound alone decides.
No kernel may reach another device: no remote copies, remote signals or barrier semaphores. Data moves between devices by JAX's collectives and lax.ppermute only.
A program may use at most 128 MiB of HBM per device.

```python
import jax
import jax.numpy as jnp
from jax import lax

FIELDS = 5
CATS = 8
NZ = 64
NY = 512
NX = 64


def draw_column_ops(key, part):
    key_diag, key_off = jax.random.split(key)
    diag = jax.random.uniform(key_diag, (FIELDS, CATS, NZ), jnp.float32, 0.6, 1.0)
    off = jnp.clip(jax.random.normal(key_off, (FIELDS, CATS, NZ, NZ), jnp.float32), -4.0, 4.0)
    off = off * (0.5 / NZ ** 0.5)
    eye = jnp.eye(NZ, dtype=jnp.float32)
    return off * (1.0 - eye) + diag[..., None] * eye


def place_ends(entries, key, least, largest):
    longest = entries.shape.index(max(entries.shape))
    spots = []
    for shift in (0, 1):
        where = [jax.random.randint(jax.random.fold_in(key, axis), (), 0, length) for axis, length in enumerate(entries.shape)]
        where[longest] = (where[longest] + shift) % entries.shape[longest]
        spots.append(tuple(where))
    return entries.at[spots[0]].set(least).at[spots[1]].set(largest)


def block_levels(key, shape, pieces, least, top_value):
    def one(axis_at, shards_of):
        draws = jax.random.uniform(jax.random.fold_in(jax.random.fold_in(key, 6), axis_at), (shards_of,), jnp.float32, least / len(pieces), top_value / len(pieces))
        return jnp.repeat(jnp.exp(draws), shape[axis_at] // shards_of).reshape((-1,) + (1,) * (len(shape) - axis_at - 1))

    loudness = one(*pieces[0])
    for cut in pieces[1:]:
        loudness = loudness * one(*cut)
    return loudness


def gaussian(stream_key, shape, spread, bound, cuts=(), held_as=jnp.bfloat16):
    array = jax.random.normal(stream_key, shape, jnp.float32) * spread
    if len(cuts) > 0:
        array = block_levels(stream_key, shape, cuts, -0.22, 0.18) * array
    return jnp.clip(array, min=-bound, max=bound).astype(held_as)


def setup_inputs(seed: int = 0) -> dict:
    streams_of = jax.random.split(jax.random.key(seed), 4)
    fields = gaussian(streams_of[0], (NZ, FIELDS, NX, NY), 1.0, 4.0, ((0, 4), (2, 8)), jnp.float32)
    land_use = place_ends(jax.random.randint(streams_of[1], (NX, NY), 0, CATS), jax.random.fold_in(streams_of[1], 1), 0, CATS - 1).astype(jnp.int32)
    column_ops = draw_column_ops(jax.random.fold_in(streams_of[3], 71), 0)
    return dict(fields=fields, land_use=land_use, column_ops=column_ops)


COURANT = 0.4


def tendency(state):
    u_wind = state[:, 2:3]
    v_wind = state[:, 3:4]
    face_x = (7.0 * (state[:, :, 1:-2] + state[:, :, 2:-1]) - (state[:, :, :-3] + state[:, :, 3:])) / 12.0
    flux_x = 0.5 * (u_wind[:, :, 1:-2] + u_wind[:, :, 2:-1]) * face_x
    div_x = flux_x[:, :, 1:] - flux_x[:, :, :-1]
    inner = state[:, :, 2:-2]
    v_inner = v_wind[:, :, 2:-2]
    face_y = (7.0 * (inner + jnp.roll(inner, -1, axis=3)) - (jnp.roll(inner, 1, axis=3) + jnp.roll(inner, -2, axis=3))) / 12.0
    flux_y = 0.5 * (v_inner + jnp.roll(v_inner, -1, axis=3)) * face_y
    div_y = flux_y - jnp.roll(flux_y, 1, axis=3)
    return -COURANT * (div_x + div_y)


def wrap_rows(state):
    return jnp.concatenate([state[:, :, -2:], state, state[:, :, :2]], axis=2)


def reference(fields, land_use, column_ops):
    current = fields
    for coef in (1.0 / 3.0, 0.5, 1.0):
        current = fields + coef * tendency(wrap_rows(current))
    outs = []
    for field in range(FIELDS):
        column = current[:, field]
        mixed = jnp.zeros_like(column)
        for cat in range(CATS):
            chosen = (land_use == cat).astype(jnp.float32)
            mixed = mixed + chosen * jnp.einsum("ij,jxy->ixy", column_ops[field, cat], column, precision=lax.Precision.HIGHEST)
        outs.append(mixed)
    return jnp.stack(outs, axis=1)
```

```python
import functools

import jax
import jax.numpy as jnp
from jax import lax
from jax.experimental import pallas as pl
from jax.experimental.pallas import tpu as pltpu
from jax.sharding import PartitionSpec as P

COURANT = 0.4
COEFS = (1.0 / 3.0, 0.5, 1.0)
CHUNKS = ((2, 3), (0,), (1,), (4,))
HALO = 6
UNROLL = 4
VMEM = pl.BlockSpec(memory_space=pltpu.VMEM)
PARAMS = pltpu.CompilerParams(vmem_limit_bytes=14 * 2**20)
F32 = jnp.float32


def cost(flops, arrays):
    size = sum(a.size * a.dtype.itemsize for a in arrays)
    return pl.CostEstimate(flops=int(flops), bytes_accessed=int(size), transcendentals=0)


def sds(*shape, dtype=F32):
    return jax.ShapeDtypeStruct(shape, dtype)


def prep_kernel(chunk, x_ref, keep_ref, send_ref):
    rows, _, half, _ = keep_ref.shape
    odd = lax.rem(lax.axis_index("tile"), 2)
    for n, f in enumerate(chunk):
        kept = jnp.swapaxes(x_ref[pl.ds(odd * half, half), f], 0, 1)
        sent = jnp.swapaxes(x_ref[pl.ds((1 - odd) * half, half), f], 0, 1)
        for r in range(rows):
            turned = jnp.where(odd == 0, r, rows - 1 - r)
            keep_ref[turned, n] = kept[r]
            send_ref[rows - 1 - turned, n] = sent[r]


def roll(a, shift):
    return pltpu.roll(a, shift % a.shape[1], 1)


def in_groups(first, end, rows, state):
    if UNROLL is None:
        return rows(first, end - first, state)

    def body(step, state):
        return rows(first + step * UNROLL, UNROLL, state)

    return lax.fori_loop(0, (end - first) // UNROLL, body, state)


def stage_rows(first, last, base, off_base, old, off_old, new, off_new, faces, fields, scales):
    ux, vr, vl = faces

    def wind(i):
        if scales is not None:
            ux[i - first + 1] = (old[off_old + i, 0] + old[off_old + i + 1, 0]) * scales[0]
        return ux[i - first + 1]

    def face(i, n, u):
        near = old[off_old + i, n] + old[off_old + i + 1, n]
        far = old[off_old + i - 1, n] + old[off_old + i + 2, n]
        return u * (7.0 * near - far)

    def rows(low, count, flux):
        flux = list(flux)
        for more in range(count):
            i = low + more
            u = wind(i)
            for n in range(fields)[::-1]:
                s = old[off_old + i, n]
                l1, l2, r1, r2 = roll(s, 1), roll(s, 2), roll(s, -1), roll(s, -2)
                left, right = s + l1, s + r1
                if scales is not None and n == 1:
                    vr[i - first] = right * scales[1]
                    vl[i - first] = left * scales[1]
                wide = vr[i - first] * (7.0 * right - (l1 + r2)) - vl[i - first] * (7.0 * left - (l2 + r1))
                here = face(i, n, u)
                new[off_new + i, n] = base[off_base + i, n] + ((here - flux[n]) + wide)
                flux[n] = here
        return tuple(flux)

    u = wind(first - 1)
    in_groups(first, last + 1, rows, tuple(face(first - 1, n, u) for n in range(fields)))


def gather_rows(parts, ext):
    at = 0
    for part in parts:
        for i in range(part.shape[0]):
            ext[at + i] = part[i]
        at += part.shape[0]


def scatter_blocks(adv, outs, lev_count, own):
    lev = lax.axis_index("lev")
    for a in range(lev_count):
        there = lev ^ a
        for q in range(own):
            outs[2 * a][q] = adv[there * own + q]
            outs[2 * a + 1][q] = adv[2 * lev_count * own - 1 - there * own - q]


def advect_kernel(lev_count, winds, before, keep, recv, after, *refs):
    rows = 2 * keep.shape[0]
    own = keep.shape[0] // lev_count
    faces, outs = refs[:9], refs[9 : 9 + 2 * lev_count]
    ext, s1, s2, adv = refs[9 + 2 * lev_count :]
    gather_rows((before, keep, recv, after), ext)
    sign = jnp.where(lax.rem(lax.axis_index("tile"), 2) == 0, 1.0, -1.0).astype(F32)
    states = ((ext, HALO), (s1, HALO - 2), (s2, HALO - 4), (adv, 0))
    for k, coef in enumerate(COEFS):
        reach = HALO - 2 * (k + 1)
        scale = -COURANT * coef / 24.0
        stage_rows(
            -reach, rows - 1 + reach, ext, HALO, *states[k], *states[k + 1],
            faces[3 * k : 3 * k + 3], keep.shape[1], (sign * scale, scale) if winds else None,
        )
    scatter_blocks(adv, outs, lev_count, own)


def advect(parts, faces, lev_count):
    keep = parts[1]
    tile_rows, fields, half, ny = keep.shape
    rows = 2 * tile_rows
    own = tile_rows // lev_count
    block = sds(own, fields, half, ny)
    sizes = [rows + 2 * (HALO - 2 * (k + 1)) for k in range(3)]
    scratch = [pltpu.VMEM((n, fields, half, ny), F32) for n in (rows + 2 * HALO, *sizes[:2], rows)]
    blocks = [block] * (2 * lev_count)
    outs, args = blocks, parts
    if faces is None:
        outs = [sds(n, half, ny) for size in sizes for n in (size + 1, size, size)] + blocks
    else:
        args = (*parts, *faces)
    return pl.pallas_call(
        functools.partial(advect_kernel, lev_count, faces is None),
        out_shape=outs,
        in_specs=[VMEM] * len(args),
        out_specs=[VMEM] * len(outs),
        scratch_shapes=scratch,
        compiler_params=PARAMS,
        cost_estimate=cost(sum(sizes) * fields * half * ny * 30, args),
    )(*args)


def mix_kernel(lev_count, use_ref, ops_ref, *refs):
    blocks, outs = refs[: 2 * lev_count], refs[2 * lev_count : 3 * lev_count]
    data, split, result = refs[3 * lev_count :]
    own, fields, half, ny = blocks[0].shape
    levels, per = data.shape[0], 2 * half
    cats = ops_ref.shape[1] // levels
    lev = lax.axis_index("lev")
    odd = lax.rem(lax.axis_index("tile"), 2)
    use = []
    for q in range(own):
        row = lev * own + q
        row = jnp.where(odd == 0, row, use_ref.shape[0] - 1 - row)
        use.append(use_ref[pl.ds(row, 1), :])
    for n in range(fields):
        for a in range(lev_count):
            for b in range(2):
                part = odd if b == 0 else 1 - odd
                at = pl.multiple_of((lev ^ a) * per + part * half, 8)
                for q in range(own):
                    data[pl.ds(at, half), q * ny : (q + 1) * ny] = blocks[2 * a + b][q, n]
        whole = data[...]
        high = whole.astype(jnp.bfloat16)
        split[0:levels] = high
        split[levels : 2 * levels] = high
        split[2 * levels :] = (whole - high.astype(F32)).astype(jnp.bfloat16)
        for q in range(own):
            for col in range(0, ny, 256):
                cols = slice(q * ny + col, q * ny + col + 256)
                every = jnp.dot(ops_ref[n], split[:, cols], preferred_element_type=F32)
                here = use[q][:, col : col + 256]
                mixed = every[:levels]
                for c in range(1, cats):
                    mixed = jnp.where(here == c, every[c * levels : (c + 1) * levels], mixed)
                result[:, cols] = mixed
        for a in range(lev_count):
            at = pl.multiple_of((lev ^ a) * per, 8)
            for q in range(own):
                outs[a][q, n] = result[pl.ds(at, per), q * ny : (q + 1) * ny]


def mix(use, ops, blocks, lev_count):
    own, fields, half, ny = blocks[0].shape
    levels = ops.shape[2] // 3
    return pl.pallas_call(
        functools.partial(mix_kernel, lev_count),
        out_shape=[sds(own, fields, 2 * half, ny)] * lev_count,
        in_specs=[VMEM] * (2 + len(blocks)),
        out_specs=[VMEM] * lev_count,
        scratch_shapes=[
            pltpu.VMEM((levels, own * ny), F32),
            pltpu.VMEM((3 * levels, own * ny), jnp.bfloat16),
            pltpu.VMEM((levels, own * ny), F32),
        ],
        compiler_params=PARAMS,
        cost_estimate=cost(2 * fields * ops.shape[1] * ops.shape[2] * own * ny, blocks),
    )(use, ops, *blocks)


def final_kernel(lev_count, *refs):
    out, turn = refs[-2:]
    lev = lax.axis_index("lev")
    odd = lax.rem(lax.axis_index("tile"), 2)
    for c, chunk in enumerate(CHUNKS):
        for n, f in enumerate(chunk):
            for a in range(lev_count):
                block = refs[c * lev_count + a]
                own = block.shape[0]
                for q in range(own):
                    row = (lev ^ a) * own + q
                    row = jnp.where(odd == 0, row, own * lev_count - 1 - row)
                    turn[row] = block[q, n]
            for low in range(0, out.shape[0], 8):
                out[low : low + 8, f] = jnp.swapaxes(turn[:, low : low + 8], 0, 1)


def per_device(fields, land_use, column_ops):
    lev_count, tile_count = lax.axis_size("lev"), lax.axis_size("tile")
    depth, total, rows, ny = fields.shape
    half = depth // 2
    levels = column_ops.shape[2]

    def send(array, target):
        pairs = [
            (lev * tile_count + tile, there * tile_count + to)
            for lev in range(lev_count)
            for tile in range(tile_count)
            for there, to in [target(lev, tile)]
        ]
        return lax.ppermute(array, ("lev", "tile"), pairs)

    def outward(lev, tile):
        return lev, (tile + (2 if tile % 2 else -2)) % tile_count

    def inward(lev, tile):
        return lev, (tile + (-2 if tile % 2 else 2)) % tile_count

    def other(lev, tile):
        return lev, tile ^ 1

    halves = []
    for chunk in CHUNKS:
        shape = sds(rows, len(chunk), half, ny)
        halves.append(
            pl.pallas_call(
                functools.partial(prep_kernel, chunk),
                out_shape=[shape, shape],
                in_specs=[VMEM],
                out_specs=[VMEM, VMEM],
                compiler_params=PARAMS,
                cost_estimate=cost(shape.size * 2, [shape] * 4),
            )(fields)
        )
    ops = column_ops.reshape(total, -1, levels)
    high = lax.reduce_precision(ops, 8, 7)
    ops = jnp.concatenate([high, ops - high, high], axis=2).astype(jnp.bfloat16)

    parts = []
    for keep, away in halves:
        recv = send(away, other)
        after = send(keep[:HALO], outward)
        before = send(recv[rows - HALO :], inward)
        parts.append((before, keep, recv, after))

    faces = None
    returned = []
    for chunk, part in zip(CHUNKS, parts):
        outs = advect(part, faces, lev_count)
        if faces is None:
            faces, outs = outs[:9], outs[9:]
        blocks = []
        for a in range(lev_count):
            for b in range(2):
                blocks.append(
                    send(outs[2 * a + b], lambda lev, tile: (lev ^ a, tile ^ b)) if a + b else outs[0]
                )
        own_ops = jnp.stack([ops[f] for f in chunk])
        mixed = mix(land_use, own_ops, blocks, lev_count)
        for a in range(lev_count):
            returned.append(send(mixed[a], lambda lev, tile: (lev ^ a, tile)) if a else mixed[0])

    return pl.pallas_call(
        functools.partial(final_kernel, lev_count),
        out_shape=sds(*fields.shape),
        in_specs=[VMEM] * len(returned),
        out_specs=VMEM,
        scratch_shapes=[pltpu.VMEM((rows, depth, ny), F32)],
        compiler_params=PARAMS,
        cost_estimate=cost(fields.size, returned + returned),
    )(*returned)


def solution(mesh):
    in_specs = (P("lev", None, "tile", None), P("tile", None), P())
    out_specs = P("lev", None, "tile", None)
    return jax.shard_map(
        per_device, mesh=mesh, in_specs=in_specs, out_specs=out_specs, check_vma=False
    )
```

```python
import functools

import jax
import jax.numpy as jnp
from jax import lax
from jax.experimental import pallas as pl
from jax.experimental.pallas import tpu as pltpu
from jax.sharding import PartitionSpec as P

COURANT = 0.4
COEFS = (1.0 / 3.0, 0.5, 1.0)
CHUNKS = ((2, 3, 0), (1, 4))
HALO = 6
UNROLL = 4
VMEM = pl.BlockSpec(memory_space=pltpu.VMEM)
PARAMS = pltpu.CompilerParams(vmem_limit_bytes=14 * 2**20)
F32 = jnp.float32


def cost(flops, arrays):
    size = sum(a.size * a.dtype.itemsize for a in arrays)
    return pl.CostEstimate(flops=int(flops), bytes_accessed=int(size), transcendentals=0)


def sds(*shape, dtype=F32):
    return jax.ShapeDtypeStruct(shape, dtype)


def prep_kernel(chunk, x_ref, keep_ref, send_ref, edge_ref, buf, sem):
    rows, _, half, _ = keep_ref.shape
    odd = lax.rem(lax.axis_index("tile"), 2)
    copies = [pltpu.make_async_copy(x_ref.at[:, f], buf.at[n], sem.at[n]) for n, f in enumerate(chunk)]
    for copy in copies:
        copy.start()
    for n, copy in enumerate(copies):
        copy.wait()
        kept = jnp.swapaxes(buf[n, pl.ds(odd * half, half)], 0, 1)
        sent = jnp.swapaxes(buf[n, pl.ds((1 - odd) * half, half)], 0, 1)
        for r in range(rows):
            turned = jnp.where(odd == 0, r, rows - 1 - r)
            keep_ref[turned, n] = kept[r]
            send_ref[rows - 1 - turned, n] = sent[r]
    for r in range(HALO):
        edge_ref[r] = keep_ref[r]


def prep(fields, chunk):
    depth, _, rows, ny = fields.shape
    shape = sds(rows, len(chunk), depth // 2, ny)
    return pl.pallas_call(
        functools.partial(prep_kernel, chunk),
        out_shape=[shape, shape, sds(HALO, *shape.shape[1:])],
        in_specs=[pl.BlockSpec(memory_space=pltpu.HBM)],
        out_specs=[VMEM] * 3,
        scratch_shapes=[
            pltpu.VMEM((len(chunk), depth, rows, ny), F32),
            pltpu.SemaphoreType.DMA((len(chunk),)),
        ],
        compiler_params=PARAMS,
        cost_estimate=cost(shape.size * 2, [shape] * 4),
    )(fields)


def ops_kernel(per, ops_ref, out_ref):
    total, cats, levels, _ = ops_ref.shape
    core = lax.rem(lax.axis_index("lev"), 2)
    line = lax.broadcasted_iota(jnp.int32, (levels, 3 * levels), 0)
    column = lax.broadcasted_iota(jnp.int32, (levels, 3 * levels), 1)
    outer = ((column == line) | (column == line + 2 * levels)).astype(jnp.bfloat16)
    middle = (column == line + levels).astype(jnp.bfloat16)
    for f in range(total):
        rows = []
        for cat in range(cats):
            for low in range(0, levels, 2 * per):
                rows.append(ops_ref[f, cat, pl.ds(pl.multiple_of(low + core * per, 8), per), :])
        rows = jnp.concatenate(rows, axis=0)
        high = rows.astype(jnp.bfloat16)
        low = (rows - high.astype(F32)).astype(jnp.bfloat16)
        spread = jnp.dot(high, outer, preferred_element_type=F32)
        spread = spread + jnp.dot(low, middle, preferred_element_type=F32)
        out_ref[f] = spread.astype(jnp.bfloat16)


def lay_ops(column_ops, per):
    total, cats, levels, _ = column_ops.shape
    out = sds(total, cats * levels // 2, 3 * levels, dtype=jnp.bfloat16)
    return pl.pallas_call(
        functools.partial(ops_kernel, per),
        out_shape=out,
        in_specs=[VMEM],
        out_specs=VMEM,
        compiler_params=PARAMS,
        cost_estimate=cost(out.size, [out, column_ops]),
    )(column_ops)


def edge_kernel(recv_ref, *refs):
    out = refs[-1]
    for r in range(HALO):
        out[r] = recv_ref[recv_ref.shape[0] - HALO + r]


def edge(recv, *earlier):
    shape = sds(HALO, *recv.shape[1:])
    return pl.pallas_call(
        edge_kernel,
        out_shape=shape,
        in_specs=[VMEM] + [pl.BlockSpec(memory_space=pl.ANY)] * len(earlier),
        out_specs=VMEM,
        compiler_params=PARAMS,
        cost_estimate=cost(0, [shape] * 2),
    )(recv, *earlier)


def later_kernel(*refs):
    pass


def later(arrays, other):
    count = len(arrays)
    return list(
        pl.pallas_call(
            later_kernel,
            out_shape=[sds(*array.shape) for array in arrays],
            in_specs=[VMEM] * count + [pl.BlockSpec(memory_space=pl.ANY)],
            out_specs=[VMEM] * count,
            input_output_aliases={n: n for n in range(count)},
            compiler_params=PARAMS,
        )(*arrays, other)
    )


def roll(a, shift):
    return pltpu.roll(a, shift % a.shape[1], 1)


def in_groups(first, end, rows, state):
    if UNROLL is None:
        return rows(first, end - first, state)

    def body(step, state):
        return rows(first + step * UNROLL, UNROLL, state)

    return lax.fori_loop(0, (end - first) // UNROLL, body, state)


def stage_rows(first, last, base, off_base, old, off_old, new, off_new, faces, fields, scales):
    ux, vr, vl = faces

    def wind(i):
        if scales is not None:
            ux[i - first + 1] = (old[off_old + i, 0] + old[off_old + i + 1, 0]) * scales[0]
        return ux[i - first + 1]

    def face(i, n, u):
        near = old[off_old + i, n] + old[off_old + i + 1, n]
        far = old[off_old + i - 1, n] + old[off_old + i + 2, n]
        return u * (7.0 * near - far)

    def rows(low, count, flux):
        flux = list(flux)
        for more in range(count):
            i = low + more
            u = wind(i)
            for n in range(fields) if scales is None else (1, 0, *range(2, fields)):
                s = old[off_old + i, n]
                l1, l2, r1, r2 = roll(s, 1), roll(s, 2), roll(s, -1), roll(s, -2)
                left, right = s + l1, s + r1
                if scales is not None and n == 1:
                    vr[i - first] = right * scales[1]
                    vl[i - first] = left * scales[1]
                wide = vr[i - first] * (7.0 * right - (l1 + r2)) - vl[i - first] * (7.0 * left - (l2 + r1))
                here = face(i, n, u)
                new[off_new + i, n] = base[off_base + i, n] + ((here - flux[n]) + wide)
                flux[n] = here
        return tuple(flux)

    u = wind(first - 1)
    in_groups(first, last + 1, rows, tuple(face(first - 1, n, u) for n in range(fields)))


def gather_rows(parts, ext):
    at = 0
    for part in parts:
        for i in range(part.shape[0]):
            ext[at + i] = part[i]
        at += part.shape[0]


def scatter_blocks(adv, outs, chips, own):
    place = lax.axis_index("lev") // 2
    for a in range(chips):
        there = place ^ a
        for q in range(own):
            outs[2 * a][q] = adv[there * own + q]
            outs[2 * a + 1][q] = adv[2 * chips * own - 1 - there * own - q]


def advect_kernel(chips, winds, before, keep, recv, after, *refs):
    rows = 2 * keep.shape[0]
    own = keep.shape[0] // chips
    faces, outs = refs[:9], refs[9 : 9 + 2 * chips]
    ext, s1, s2, adv = refs[9 + 2 * chips :]
    gather_rows((before, keep, recv, after), ext)
    sign = jnp.where(lax.rem(lax.axis_index("tile"), 2) == 0, 1.0, -1.0).astype(F32)
    states = ((ext, HALO), (s1, HALO - 2), (s2, HALO - 4), (adv, 0))
    for k, coef in enumerate(COEFS):
        reach = HALO - 2 * (k + 1)
        scale = -COURANT * coef / 24.0
        stage_rows(
            -reach, rows - 1 + reach, ext, HALO, *states[k], *states[k + 1],
            faces[3 * k : 3 * k + 3], keep.shape[1], (sign * scale, scale) if winds else None,
        )
    scatter_blocks(adv, outs, chips, own)


def advect(parts, faces, chips):
    keep = parts[1]
    tile_rows, fields, half, ny = keep.shape
    rows = 2 * tile_rows
    own = tile_rows // chips
    block = sds(own, fields, half, ny)
    sizes = [rows + 2 * (HALO - 2 * (k + 1)) for k in range(3)]
    scratch = [pltpu.VMEM((n, fields, half, ny), F32) for n in (rows + 2 * HALO, *sizes[:2], rows)]
    blocks = [block] * (2 * chips)
    outs, args = blocks, parts
    if faces is None:
        outs = [sds(n, half, ny) for size in sizes for n in (size + 1, size, size)] + blocks
    else:
        args = (*parts, *faces)
    return pl.pallas_call(
        functools.partial(advect_kernel, chips, faces is None),
        out_shape=outs,
        in_specs=[VMEM] * len(args),
        out_specs=[VMEM] * len(outs),
        scratch_shapes=scratch,
        compiler_params=PARAMS,
        cost_estimate=cost(sum(sizes) * fields * half * ny * 30, args),
    )(*args)


def mix_kernel(chips, chunk, use_ref, ops_ref, *refs):
    blocks, outs = refs[: 4 * chips], refs[4 * chips : 5 * chips]
    token, data, result = refs[5 * chips :]
    token[...] = jnp.zeros_like(token)
    own, _, half, ny = blocks[0].shape
    levels, per = data.shape[0], 2 * half
    kept = chips * per
    cats = ops_ref.shape[1] // kept
    lev = lax.axis_index("lev")
    place, core = lev // 2, lax.rem(lev, 2)
    odd = lax.rem(lax.axis_index("tile"), 2)
    use = []
    for q in range(own):
        row = place * own + q
        row = jnp.where(odd == 0, row, use_ref.shape[0] - 1 - row)
        use.append(use_ref[pl.ds(row, 1), :])
    for n, f in enumerate(chunk):
        for c in range(2):
            for a in range(chips):
                for b in range(2):
                    source = 2 * (place ^ a) + (core ^ c)
                    at = pl.multiple_of(source * per + (odd ^ b) * half, 8)
                    for q in range(own):
                        data[pl.ds(at, half), q * ny : (q + 1) * ny] = blocks[2 * chips * c + 2 * a + b][q, n]
        for q in range(own):
            for col in range(0, ny, 256):
                cols = slice(q * ny + col, q * ny + col + 256)
                whole = data[:, cols]
                high = whole.astype(jnp.bfloat16)
                low = (whole - high.astype(F32)).astype(jnp.bfloat16)
                three = jnp.concatenate([high, high, low], axis=0)
                every = jnp.dot(ops_ref[f], three, preferred_element_type=F32)
                here = use[q][:, col : col + 256]
                mixed = every[:kept]
                for c in range(1, cats):
                    mixed = jnp.where(here == c, every[c * kept : (c + 1) * kept], mixed)
                result[:, cols] = mixed
        for a in range(chips):
            at = pl.multiple_of((place ^ a) * per, 8)
            for q in range(own):
                outs[a][q, n] = result[pl.ds(at, per), q * ny : (q + 1) * ny]


def mix(chunk, use, ops, blocks, chips):
    own, fields, half, ny = blocks[0].shape
    levels = ops.shape[2] // 3
    return pl.pallas_call(
        functools.partial(mix_kernel, chips, chunk),
        out_shape=[sds(own, fields, 2 * half, ny)] * chips + [sds(8, 128)],
        in_specs=[VMEM] * (2 + len(blocks)),
        out_specs=[VMEM] * (chips + 1),
        scratch_shapes=[
            pltpu.VMEM((levels, own * ny), F32),
            pltpu.VMEM((levels // 2, own * ny), F32),
        ],
        compiler_params=PARAMS,
        cost_estimate=cost(2 * fields * ops.shape[1] * ops.shape[2] * own * ny, blocks),
    )(use, ops, *blocks)


def final_kernel(chips, chunks, *refs):
    out, turn = refs[-2:]
    place = lax.axis_index("lev") // 2
    odd = lax.rem(lax.axis_index("tile"), 2)
    for c, chunk in enumerate(chunks):
        for n, f in enumerate(chunk):
            for a in range(chips):
                block = refs[c * chips + a]
                own = block.shape[0]
                for q in range(own):
                    row = (place ^ a) * own + q
                    row = jnp.where(odd == 0, row, own * chips - 1 - row)
                    turn[row] = block[q, n]
            for low in range(0, out.shape[0], 8):
                out[low : low + 8, f] = jnp.swapaxes(turn[:, low : low + 8], 0, 1)


def per_device(fields, land_use, column_ops):
    lev_count, tile_count = lax.axis_size("lev"), lax.axis_size("tile")
    depth, total, rows, ny = fields.shape

    def send(array, target):
        pairs = [
            (lev * tile_count + tile, there * tile_count + to)
            for lev in range(lev_count)
            for tile in range(tile_count)
            for there, to in [target(lev, tile)]
        ]
        return lax.ppermute(array, ("lev", "tile"), pairs)

    def outward(lev, tile):
        return lev, (tile + (2 if tile % 2 else -2)) % tile_count

    def inward(lev, tile):
        return lev, (tile + (-2 if tile % 2 else 2)) % tile_count

    def other(lev, tile):
        return lev, tile ^ 1

    chips = lev_count // 2
    ops = lay_ops(column_ops, depth)

    def outspread(outs):
        return [
            send(outs[2 * a + b], lambda lev, tile: (lev ^ 2 * a, tile ^ b)) if a + b else outs[0]
            for a in range(chips)
            for b in range(2)
        ]

    def both_cores(blocks):
        return blocks + [send(block, lambda lev, tile: (lev ^ 1, tile)) for block in blocks]

    def mixed_back(chunk, blocks):
        mixed = mix(chunk, land_use, ops, blocks, chips)
        back = [send(mixed[a], lambda lev, tile: (lev ^ 2 * a, tile)) if a else mixed[0] for a in range(chips)]
        return back, mixed[-1]

    first, second = CHUNKS
    keep_a, away_a, edge_a = prep(fields, first)
    recv_a = send(away_a, other)
    after_a = send(edge_a, outward)
    keep_b, away_b, edge_b = prep(fields, second)
    recv_a, away_b, edge_b = lax.optimization_barrier((recv_a, away_b, edge_b))
    before_a = send(edge(recv_a), inward)
    recv_b = send(away_b, other)
    after_b = send(edge_b, outward)
    outs_a = advect((before_a, keep_a, recv_a, after_a), None, chips)
    faces, outs_a = outs_a[:9], outs_a[9:]
    blocks_a = outspread(outs_a)
    before_b = send(edge(recv_b, before_a), inward)
    outs_b = advect((before_b, keep_b, recv_b, after_b), faces, chips)
    blocks_b = outspread(outs_b)
    returned, mixed = mixed_back(first, both_cores(blocks_a))
    blocks_b = later(blocks_b, mixed)
    returned += mixed_back(second, both_cores(blocks_b))[0]

    return pl.pallas_call(
        functools.partial(final_kernel, chips, CHUNKS),
        out_shape=sds(*fields.shape),
        in_specs=[VMEM] * len(returned),
        out_specs=VMEM,
        scratch_shapes=[pltpu.VMEM((rows, depth, ny), F32)],
        compiler_params=PARAMS,
        cost_estimate=cost(fields.size, returned + returned),
    )(*returned)


def solution(mesh):
    in_specs = (P("lev", None, "tile", None), P("tile", None), P())
    out_specs = P("lev", None, "tile", None)
    return jax.shard_map(
        per_device, mesh=mesh, in_specs=in_specs, out_specs=out_specs, check_vma=False
    )
```

```python
import functools

import jax
import jax.numpy as jnp
from jax import lax
from jax.experimental import pallas as pl
from jax.experimental.pallas import tpu as pltpu
from jax.sharding import PartitionSpec as P

COURANT = 0.4
COEFS = (1.0 / 3.0, 0.5, 1.0)
CHUNKS = ((2, 3, 0), (1, 4))
HALO = 6
UNROLL = 4
VMEM = pl.BlockSpec(memory_space=pltpu.VMEM)
PARAMS = pltpu.CompilerParams(vmem_limit_bytes=14 * 2**20)
F32 = jnp.float32


def cost(flops, arrays):
    return pl.CostEstimate(flops=1, bytes_accessed=1, transcendentals=0)


def sds(*shape, dtype=F32):
    return jax.ShapeDtypeStruct(shape, dtype)


def prep_kernel(chunk, x_ref, keep_ref, send_ref, near_ref, far_ref, buf, sem):
    rows, _, half, _ = keep_ref.shape
    odd = lax.rem(lax.axis_index("tile"), 2)
    copies = [pltpu.make_async_copy(x_ref.at[:, f], buf.at[n], sem.at[n]) for n, f in enumerate(chunk)]
    for copy in copies:
        copy.start()
    for n, copy in enumerate(copies):
        copy.wait()
        kept = jnp.swapaxes(buf[n, pl.ds(odd * half, half)], 0, 1)
        sent = jnp.swapaxes(buf[n, pl.ds((1 - odd) * half, half)], 0, 1)
        for r in range(rows):
            turned = jnp.where(odd == 0, r, rows - 1 - r)
            keep_ref[turned, n] = kept[r]
            send_ref[rows - 1 - turned, n] = sent[r]
    for r in range(HALO):
        near_ref[r] = keep_ref[r]
        far_ref[r] = send_ref[rows - HALO + r]


def prep(fields, chunk):
    depth, _, rows, ny = fields.shape
    shape = sds(rows, len(chunk), depth // 2, ny)
    return pl.pallas_call(
        functools.partial(prep_kernel, chunk),
        out_shape=[shape, shape] + [sds(HALO, *shape.shape[1:])] * 2,
        in_specs=[pl.BlockSpec(memory_space=pltpu.HBM)],
        out_specs=[VMEM] * 4,
        scratch_shapes=[
            pltpu.VMEM((len(chunk), depth, rows, ny), F32),
            pltpu.SemaphoreType.DMA((len(chunk),)),
        ],
        compiler_params=PARAMS,
        cost_estimate=cost(shape.size * 2, [shape] * 4),
    )(fields)


def ops_kernel(per, ops_ref, out_ref):
    total, cats, levels, _ = ops_ref.shape
    core = lax.rem(lax.axis_index("lev"), 2)
    line = lax.broadcasted_iota(jnp.int32, (levels, 3 * levels), 0)
    column = lax.broadcasted_iota(jnp.int32, (levels, 3 * levels), 1)
    outer = ((column == line) | (column == line + 2 * levels)).astype(jnp.bfloat16)
    middle = (column == line + levels).astype(jnp.bfloat16)
    for f in range(total):
        rows = []
        for cat in range(cats):
            for low in range(0, levels, 2 * per):
                rows.append(ops_ref[f, cat, pl.ds(pl.multiple_of(low + core * per, 8), per), :])
        rows = jnp.concatenate(rows, axis=0)
        high = rows.astype(jnp.bfloat16)
        low = (rows - high.astype(F32)).astype(jnp.bfloat16)
        spread = jnp.dot(high, outer, preferred_element_type=F32)
        spread = spread + jnp.dot(low, middle, preferred_element_type=F32)
        out_ref[f] = spread.astype(jnp.bfloat16)


def lay_ops(column_ops, per):
    total, cats, levels, _ = column_ops.shape
    out = sds(total, cats * levels // 2, 3 * levels, dtype=jnp.bfloat16)
    return pl.pallas_call(
        functools.partial(ops_kernel, per),
        out_shape=out,
        in_specs=[VMEM],
        out_specs=VMEM,
        compiler_params=PARAMS,
        cost_estimate=cost(out.size, [out, column_ops]),
    )(column_ops)


def later_kernel(*refs):
    pass


def later(arrays, *others):
    count = len(arrays)
    return list(
        pl.pallas_call(
            later_kernel,
            out_shape=[sds(*array.shape) for array in arrays],
            in_specs=[VMEM] * count + [pl.BlockSpec(memory_space=pl.ANY)] * len(others),
            out_specs=[VMEM] * count,
            input_output_aliases={n: n for n in range(count)},
            compiler_params=PARAMS,
        )(*arrays, *others)
    )


def roll(a, shift):
    return pltpu.roll(a, shift % a.shape[1], 1)


def in_groups(first, end, rows, state):
    if UNROLL is None:
        return rows(first, end - first, state)

    def body(step, state):
        return rows(first + step * UNROLL, UNROLL, state)

    return lax.fori_loop(0, (end - first) // UNROLL, body, state)


def stage_rows(first, last, base, off_base, old, off_old, new, off_new, faces, fields, scales):
    ux, vr, vl = faces

    def wind(i):
        if scales is not None:
            ux[i - first + 1] = (old[off_old + i, 0] + old[off_old + i + 1, 0]) * scales[0]
        return ux[i - first + 1]

    def face(i, n, u):
        near = old[off_old + i, n] + old[off_old + i + 1, n]
        far = old[off_old + i - 1, n] + old[off_old + i + 2, n]
        return u * (7.0 * near - far)

    def rows(low, count, flux):
        flux = list(flux)
        for more in range(count):
            i = low + more
            u = wind(i)
            for n in range(fields) if scales is None else (1, 0, *range(2, fields)):
                s = old[off_old + i, n]
                l1, l2, r1, r2 = roll(s, 1), roll(s, 2), roll(s, -1), roll(s, -2)
                left, right = s + l1, s + r1
                if scales is not None and n == 1:
                    vr[i - first] = right * scales[1]
                    vl[i - first] = left * scales[1]
                wide = vr[i - first] * (7.0 * right - (l1 + r2)) - vl[i - first] * (7.0 * left - (l2 + r1))
                here = face(i, n, u)
                new[off_new + i, n] = base[off_base + i, n] + ((here - flux[n]) + wide)
                flux[n] = here
        return tuple(flux)

    u = wind(first - 1)
    in_groups(first, last + 1, rows, tuple(face(first - 1, n, u) for n in range(fields)))


def gather_rows(parts, ext):
    at = 0
    for part in parts:
        for i in range(part.shape[0]):
            ext[at + i] = part[i]
        at += part.shape[0]


def scatter_blocks(adv, outs, chips, own):
    place = lax.axis_index("lev") // 2
    for a in range(chips):
        there = place ^ a
        for q in range(own):
            outs[2 * a][q] = adv[there * own + q]
            outs[2 * a + 1][q] = adv[2 * chips * own - 1 - there * own - q]


def advect_kernel(chips, winds, before, keep, recv, after, *refs):
    rows = 2 * keep.shape[0]
    own = keep.shape[0] // chips
    faces, outs = refs[:9], refs[9 : 9 + 2 * chips]
    ext, s1, s2, adv = refs[9 + 2 * chips :]
    gather_rows((before, keep, recv, after), ext)
    sign = jnp.where(lax.rem(lax.axis_index("tile"), 2) == 0, 1.0, -1.0).astype(F32)
    states = ((ext, HALO), (s1, HALO - 2), (s2, HALO - 4), (adv, 0))
    for k, coef in enumerate(COEFS):
        reach = HALO - 2 * (k + 1)
        scale = -COURANT * coef / 24.0
        stage_rows(
            -reach, rows - 1 + reach, ext, HALO, *states[k], *states[k + 1],
            faces[3 * k : 3 * k + 3], keep.shape[1], (sign * scale, scale) if winds else None,
        )
    scatter_blocks(adv, outs, chips, own)


def advect(parts, faces, chips):
    keep = parts[1]
    tile_rows, fields, half, ny = keep.shape
    rows = 2 * tile_rows
    own = tile_rows // chips
    block = sds(own, fields, half, ny)
    sizes = [rows + 2 * (HALO - 2 * (k + 1)) for k in range(3)]
    scratch = [pltpu.VMEM((n, fields, half, ny), F32) for n in (rows + 2 * HALO, *sizes[:2], rows)]
    blocks = [block] * (2 * chips)
    outs, args = blocks, parts
    if faces is None:
        outs = [sds(n, half, ny) for size in sizes for n in (size + 1, size, size)] + blocks
    else:
        args = (*parts, *faces)
    return pl.pallas_call(
        functools.partial(advect_kernel, chips, faces is None),
        out_shape=outs,
        in_specs=[VMEM] * len(args),
        out_specs=[VMEM] * len(outs),
        scratch_shapes=scratch,
        compiler_params=PARAMS,
        cost_estimate=cost(sum(sizes) * fields * half * ny * 30, args),
    )(*args)


def mix_kernel(chips, chunk, use_ref, ops_ref, *refs):
    blocks, outs = refs[: 4 * chips], refs[4 * chips + 1 : 5 * chips + 1]
    data, result = refs[5 * chips + 1 :]
    own, _, half, ny = blocks[0].shape
    levels, per = data.shape[0], 2 * half
    kept = chips * per
    cats = ops_ref.shape[1] // kept
    lev = lax.axis_index("lev")
    place, core = lev // 2, lax.rem(lev, 2)
    odd = lax.rem(lax.axis_index("tile"), 2)
    use = []
    for q in range(own):
        row = place * own + q
        row = jnp.where(odd == 0, row, use_ref.shape[0] - 1 - row)
        use.append(use_ref[pl.ds(row, 1), :])
    for n, f in enumerate(chunk):
        for c in range(2):
            for a in range(chips):
                for b in range(2):
                    source = 2 * (place ^ a) + (core ^ c)
                    at = pl.multiple_of(source * per + (odd ^ b) * half, 8)
                    for q in range(own):
                        data[pl.ds(at, half), q * ny : (q + 1) * ny] = blocks[2 * chips * c + 2 * a + b][q, n]
        for q in range(own):
            for col in range(0, ny, 256):
                cols = slice(q * ny + col, q * ny + col + 256)
                whole = data[:, cols]
                high = whole.astype(jnp.bfloat16)
                low = (whole - high.astype(F32)).astype(jnp.bfloat16)
                three = jnp.concatenate([high, high, low], axis=0)
                every = jnp.dot(ops_ref[f], three, preferred_element_type=F32)
                here = use[q][:, col : col + 256]
                mixed = every[:kept]
                for c in range(1, cats):
                    mixed = jnp.where(here == c, every[c * kept : (c + 1) * kept], mixed)
                result[:, cols] = mixed
        for a in range(chips):
            at = pl.multiple_of((place ^ a) * per, 8)
            for q in range(own):
                outs[a][q, n] = result[pl.ds(at, per), q * ny : (q + 1) * ny]


def mix(chunk, use, ops, blocks, earlier, chips):
    own, fields, half, ny = blocks[0].shape
    levels = ops.shape[2] // 3
    return pl.pallas_call(
        functools.partial(mix_kernel, chips, chunk),
        out_shape=[sds(own, fields, 2 * half, ny)] * chips,
        in_specs=[VMEM] * (2 + len(blocks)) + [pl.BlockSpec(memory_space=pl.ANY)],
        out_specs=[VMEM] * chips,
        scratch_shapes=[
            pltpu.VMEM((levels, own * ny), F32),
            pltpu.VMEM((levels // 2, own * ny), F32),
        ],
        compiler_params=PARAMS,
        cost_estimate=cost(2 * fields * ops.shape[1] * ops.shape[2] * own * ny, blocks),
    )(use, ops, *blocks, earlier)


def final_kernel(chips, chunks, *refs):
    out, turn = refs[-2:]
    place = lax.axis_index("lev") // 2
    odd = lax.rem(lax.axis_index("tile"), 2)
    for c, chunk in enumerate(chunks):
        for n, f in enumerate(chunk):
            for a in range(chips):
                block = refs[c * chips + a]
                own = block.shape[0]
                for q in range(own):
                    row = (place ^ a) * own + q
                    row = jnp.where(odd == 0, row, own * chips - 1 - row)
                    turn[row] = block[q, n]
            for low in range(0, out.shape[0], 8):
                out[low : low + 8, f] = jnp.swapaxes(turn[:, low : low + 8], 0, 1)


def per_device(fields, land_use, column_ops):
    lev_count, tile_count = lax.axis_size("lev"), lax.axis_size("tile")
    depth, total, rows, ny = fields.shape

    def send(array, target):
        pairs = [
            (lev * tile_count + tile, there * tile_count + to)
            for lev in range(lev_count)
            for tile in range(tile_count)
            for there, to in [target(lev, tile)]
        ]
        return lax.ppermute(array, ("lev", "tile"), pairs)

    def outward(lev, tile):
        return lev, (tile + (2 if tile % 2 else -2)) % tile_count

    def across(lev, tile):
        return lev, (tile + (1 if tile % 2 else -1)) % tile_count

    def other(lev, tile):
        return lev, tile ^ 1

    chips = lev_count // 2
    ops = lay_ops(column_ops, depth)

    def outspread(outs):
        return [
            send(outs[2 * a + b], lambda lev, tile: (lev ^ 2 * a, tile ^ b)) if a + b else outs[0]
            for a in range(chips)
            for b in range(2)
        ]

    def both_cores(blocks):
        return blocks + [send(block, lambda lev, tile: (lev ^ 1, tile)) for block in blocks]

    def mixed_back(chunk, blocks, earlier):
        mixed = mix(chunk, land_use, ops, blocks, earlier, chips)
        return [send(mixed[a], lambda lev, tile: (lev ^ 2 * a, tile)) if a else mixed[0] for a in range(chips)]

    first, second = CHUNKS
    keep_a, away_a, near_a, far_a = prep(fields, first)
    recv_a = send(away_a, other)
    before_a = send(far_a, across)
    after_a = send(near_a, outward)
    keep_b, away_b, near_b, far_b = prep(fields, second)
    before_a, away_b, near_b, far_b = lax.optimization_barrier((before_a, away_b, near_b, far_b))
    recv_b = send(away_b, other)
    before_b = send(far_b, across)
    after_b = send(near_b, outward)
    outs_a = advect((before_a, keep_a, recv_a, after_a), None, chips)
    faces, outs_a = outs_a[:9], outs_a[9:]
    blocks_a = outspread(outs_a)
    outs_b = advect((before_b, keep_b, recv_b, after_b), faces, chips)
    blocks_b = outspread(outs_b)
    blocks_a = later(blocks_a, *blocks_b[1:])
    returned = mixed_back(first, both_cores(blocks_a), outs_b[0])
    returned += mixed_back(second, both_cores(blocks_b), returned[0])

    return pl.pallas_call(
        functools.partial(final_kernel, chips, CHUNKS),
        out_shape=sds(*fields.shape),
        in_specs=[VMEM] * len(returned),
        out_specs=VMEM,
        scratch_shapes=[pltpu.VMEM((rows, depth, ny), F32)],
        compiler_params=PARAMS,
        cost_estimate=cost(fields.size, returned + returned),
    )(*returned)


def solution(mesh):
    in_specs = (P("lev", None, "tile", None), P("tile", None), P())
    out_specs = P("lev", None, "tile", None)
    return jax.shard_map(
        per_device, mesh=mesh, in_specs=in_specs, out_specs=out_specs, check_vma=False
    )
```

```python
import functools

import jax
import jax.numpy as jnp
from jax import lax
from jax.experimental import pallas as pl
from jax.experimental.pallas import tpu as pltpu
from jax.sharding import PartitionSpec as P

COURANT = 0.4
COEFS = (1.0 / 3.0, 0.5, 1.0)
CHUNKS = ((2, 3, 4), (0, 1))
HALO = 6
UNROLL = 4
VMEM = pl.BlockSpec(memory_space=pltpu.VMEM)
PARAMS = pltpu.CompilerParams(vmem_limit_bytes=14 * 2**20)
F32 = jnp.float32


def cost(flops, arrays):
    return pl.CostEstimate(flops=1, bytes_accessed=1, transcendentals=0)


def sds(*shape, dtype=F32):
    return jax.ShapeDtypeStruct(shape, dtype)


def prep_kernel(x_ref, keep_ref, send_ref, near_ref, far_ref):
    rows, _, half, _ = keep_ref.shape
    odd = lax.rem(lax.axis_index("tile"), 2)
    for n in range(keep_ref.shape[1]):
        kept = jnp.swapaxes(x_ref[pl.ds(odd * half, half), n], 0, 1)
        sent = jnp.swapaxes(x_ref[pl.ds((1 - odd) * half, half), n], 0, 1)
        for r in range(rows):
            turned = jnp.where(odd == 0, r, rows - 1 - r)
            keep_ref[turned, n] = kept[r]
            send_ref[rows - 1 - turned, n] = sent[r]
    for r in range(HALO):
        near_ref[r] = keep_ref[r]
        far_ref[r] = send_ref[rows - HALO + r]


def prep(part):
    depth, count, rows, ny = part.shape
    shape = sds(rows, count, depth // 2, ny)
    return pl.pallas_call(
        prep_kernel,
        out_shape=[shape, shape] + [sds(HALO, *shape.shape[1:])] * 2,
        in_specs=[VMEM],
        out_specs=[VMEM] * 4,
        compiler_params=PARAMS,
        cost_estimate=cost(shape.size * 2, [shape] * 4),
    )(part)


def ops_kernel(per, ops_ref, out_ref):
    total, cats, levels, _ = ops_ref.shape
    core = lax.rem(lax.axis_index("lev"), 2)
    line = lax.broadcasted_iota(jnp.int32, (levels, 3 * levels), 0)
    column = lax.broadcasted_iota(jnp.int32, (levels, 3 * levels), 1)
    outer = ((column == line) | (column == line + 2 * levels)).astype(jnp.bfloat16)
    middle = (column == line + levels).astype(jnp.bfloat16)
    for f in range(total):
        rows = []
        for cat in range(cats):
            for low in range(0, levels, 2 * per):
                rows.append(ops_ref[f, cat, pl.ds(pl.multiple_of(low + core * per, 8), per), :])
        rows = jnp.concatenate(rows, axis=0)
        high = rows.astype(jnp.bfloat16)
        low = (rows - high.astype(F32)).astype(jnp.bfloat16)
        spread = jnp.dot(high, outer, preferred_element_type=F32)
        spread = spread + jnp.dot(low, middle, preferred_element_type=F32)
        out_ref[f] = spread.astype(jnp.bfloat16)


def lay_ops(column_ops, per):
    total, cats, levels, _ = column_ops.shape
    out = sds(total, cats * levels // 2, 3 * levels, dtype=jnp.bfloat16)
    return pl.pallas_call(
        functools.partial(ops_kernel, per),
        out_shape=out,
        in_specs=[VMEM],
        out_specs=VMEM,
        compiler_params=PARAMS,
        cost_estimate=cost(out.size, [out, column_ops]),
    )(column_ops)


def later_kernel(*refs):
    pass


def later(arrays, *others):
    count = len(arrays)
    return list(
        pl.pallas_call(
            later_kernel,
            out_shape=[sds(*array.shape) for array in arrays],
            in_specs=[VMEM] * count + [pl.BlockSpec(memory_space=pl.ANY)] * len(others),
            out_specs=[VMEM] * count,
            input_output_aliases={n: n for n in range(count)},
            compiler_params=PARAMS,
        )(*arrays, *others)
    )


def roll(a, shift):
    return pltpu.roll(a, shift % a.shape[1], 1)


def in_groups(first, end, rows, state):
    if UNROLL is None:
        return rows(first, end - first, state)

    def body(step, state):
        return rows(first + step * UNROLL, UNROLL, state)

    return lax.fori_loop(0, (end - first) // UNROLL, body, state)


def stage_rows(first, last, base, off_base, old, off_old, new, off_new, faces, fields, scales):
    ux, vr, vl = faces

    def wind(i):
        if scales is not None:
            ux[i - first + 1] = (old[off_old + i, 0] + old[off_old + i + 1, 0]) * scales[0]
        return ux[i - first + 1]

    def face(i, n, u):
        near = old[off_old + i, n] + old[off_old + i + 1, n]
        far = old[off_old + i - 1, n] + old[off_old + i + 2, n]
        return u * (7.0 * near - far)

    def rows(low, count, flux):
        flux = list(flux)
        for more in range(count):
            i = low + more
            u = wind(i)
            for n in range(fields) if scales is None else (1, 0, *range(2, fields)):
                s = old[off_old + i, n]
                l1, l2, r1, r2 = roll(s, 1), roll(s, 2), roll(s, -1), roll(s, -2)
                left, right = s + l1, s + r1
                if scales is not None and n == 1:
                    vr[i - first] = right * scales[1]
                    vl[i - first] = left * scales[1]
                wide = vr[i - first] * (7.0 * right - (l1 + r2)) - vl[i - first] * (7.0 * left - (l2 + r1))
                here = face(i, n, u)
                new[off_new + i, n] = base[off_base + i, n] + ((here - flux[n]) + wide)
                flux[n] = here
        return tuple(flux)

    u = wind(first - 1)
    in_groups(first, last + 1, rows, tuple(face(first - 1, n, u) for n in range(fields)))


def gather_rows(parts, ext):
    at = 0
    for part in parts:
        for i in range(part.shape[0]):
            ext[at + i] = part[i]
        at += part.shape[0]


def scatter_blocks(adv, outs, chips, own):
    place = lax.axis_index("lev") // 2
    for a in range(chips):
        there = place ^ a
        for q in range(own):
            outs[2 * a][q] = adv[there * own + q]
            outs[2 * a + 1][q] = adv[2 * chips * own - 1 - there * own - q]


def advect_kernel(chips, winds, before, keep, recv, after, *refs):
    rows = 2 * keep.shape[0]
    own = keep.shape[0] // chips
    faces, outs = refs[:9], refs[9 : 9 + 2 * chips]
    ext, s1, s2, adv = refs[9 + 2 * chips :]
    gather_rows((before, keep, recv, after), ext)
    sign = jnp.where(lax.rem(lax.axis_index("tile"), 2) == 0, 1.0, -1.0).astype(F32)
    states = ((ext, HALO), (s1, HALO - 2), (s2, HALO - 4), (adv, 0))
    for k, coef in enumerate(COEFS):
        reach = HALO - 2 * (k + 1)
        scale = -COURANT * coef / 24.0
        stage_rows(
            -reach, rows - 1 + reach, ext, HALO, *states[k], *states[k + 1],
            faces[3 * k : 3 * k + 3], keep.shape[1], (sign * scale, scale) if winds else None,
        )
    scatter_blocks(adv, outs, chips, own)


def advect(parts, faces, chips):
    keep = parts[1]
    tile_rows, fields, half, ny = keep.shape
    rows = 2 * tile_rows
    own = tile_rows // chips
    block = sds(own, fields, half, ny)
    sizes = [rows + 2 * (HALO - 2 * (k + 1)) for k in range(3)]
    scratch = [pltpu.VMEM((n, fields, half, ny), F32) for n in (rows + 2 * HALO, *sizes[:2], rows)]
    blocks = [block] * (2 * chips)
    outs, args = blocks, parts
    if faces is None:
        outs = [sds(n, half, ny) for size in sizes for n in (size + 1, size, size)] + blocks
    else:
        args = (*parts, *faces)
    return pl.pallas_call(
        functools.partial(advect_kernel, chips, faces is None),
        out_shape=outs,
        in_specs=[VMEM] * len(args),
        out_specs=[VMEM] * len(outs),
        scratch_shapes=scratch,
        compiler_params=PARAMS,
        cost_estimate=cost(sum(sizes) * fields * half * ny * 30, args),
    )(*args)


def mix_kernel(chips, chunk, use_ref, ops_ref, *refs):
    blocks, outs = refs[: 4 * chips], refs[4 * chips + 1 : 5 * chips + 1]
    data, result = refs[5 * chips + 1 :]
    own, _, half, ny = blocks[0].shape
    levels, per = data.shape[0], 2 * half
    kept = chips * per
    cats = ops_ref.shape[1] // kept
    lev = lax.axis_index("lev")
    place, core = lev // 2, lax.rem(lev, 2)
    odd = lax.rem(lax.axis_index("tile"), 2)
    use = []
    for q in range(own):
        row = place * own + q
        row = jnp.where(odd == 0, row, use_ref.shape[0] - 1 - row)
        use.append(use_ref[pl.ds(row, 1), :])
    for n, f in enumerate(chunk):
        for c in range(2):
            for a in range(chips):
                for b in range(2):
                    source = 2 * (place ^ a) + (core ^ c)
                    at = pl.multiple_of(source * per + (odd ^ b) * half, 8)
                    for q in range(own):
                        data[pl.ds(at, half), q * ny : (q + 1) * ny] = blocks[2 * chips * c + 2 * a + b][q, n]
        for q in range(own):
            for col in range(0, ny, 256):
                cols = slice(q * ny + col, q * ny + col + 256)
                whole = data[:, cols]
                high = whole.astype(jnp.bfloat16)
                low = (whole - high.astype(F32)).astype(jnp.bfloat16)
                three = jnp.concatenate([high, high, low], axis=0)
                every = jnp.dot(ops_ref[f], three, preferred_element_type=F32)
                here = use[q][:, col : col + 256]
                mixed = every[:kept]
                for c in range(1, cats):
                    mixed = jnp.where(here == c, every[c * kept : (c + 1) * kept], mixed)
                result[:, cols] = mixed
        for a in range(chips):
            at = pl.multiple_of((place ^ a) * per, 8)
            for q in range(own):
                outs[a][q, n] = result[pl.ds(at, per), q * ny : (q + 1) * ny]


def mix(chunk, use, ops, blocks, earlier, chips):
    own, fields, half, ny = blocks[0].shape
    levels = ops.shape[2] // 3
    return pl.pallas_call(
        functools.partial(mix_kernel, chips, chunk),
        out_shape=[sds(own, fields, 2 * half, ny)] * chips,
        in_specs=[VMEM] * (2 + len(blocks)) + [pl.BlockSpec(memory_space=pl.ANY)],
        out_specs=[VMEM] * chips,
        scratch_shapes=[
            pltpu.VMEM((levels, own * ny), F32),
            pltpu.VMEM((levels // 2, own * ny), F32),
        ],
        compiler_params=PARAMS,
        cost_estimate=cost(2 * fields * ops.shape[1] * ops.shape[2] * own * ny, blocks),
    )(use, ops, *blocks, earlier)


def final_kernel(chips, chunk, *refs):
    blocks, (out, turn, done, sem) = refs[:chips], refs[-4:]
    place = lax.axis_index("lev") // 2
    odd = lax.rem(lax.axis_index("tile"), 2)
    copies = []
    for n, f in enumerate(chunk):
        for a in range(chips):
            own = blocks[a].shape[0]
            for q in range(own):
                row = (place ^ a) * own + q
                row = jnp.where(odd == 0, row, own * chips - 1 - row)
                turn[row] = blocks[a][q, n]
        for low in range(0, out.shape[0], 8):
            done[n, low : low + 8] = jnp.swapaxes(turn[:, low : low + 8], 0, 1)
        copies.append(pltpu.make_async_copy(done.at[n], out.at[:, f], sem.at[n]))
        copies[-1].start()
    for copy in copies:
        copy.wait()


def final(chunk, blocks, held, shape, size):
    depth, _, rows, ny = shape
    whole = [] if held is None else [held]
    return pl.pallas_call(
        functools.partial(final_kernel, len(blocks), chunk),
        out_shape=sds(*shape),
        in_specs=[VMEM] * len(blocks) + [pl.BlockSpec(memory_space=pl.ANY)] * len(whole),
        out_specs=pl.BlockSpec(memory_space=pl.ANY),
        input_output_aliases={len(blocks): 0} if whole else {},
        scratch_shapes=[
            pltpu.VMEM((rows, depth, ny), F32),
            pltpu.VMEM((len(chunk), depth, rows, ny), F32),
            pltpu.SemaphoreType.DMA((len(chunk),)),
        ],
        compiler_params=PARAMS,
        cost_estimate=pl.CostEstimate(flops=size, bytes_accessed=1, transcendentals=0),
    )(*blocks, *whole)


def per_device(fields, land_use, column_ops):
    lev_count, tile_count = lax.axis_size("lev"), lax.axis_size("tile")
    depth, total, rows, ny = fields.shape

    def send(array, target):
        pairs = [
            (lev * tile_count + tile, there * tile_count + to)
            for lev in range(lev_count)
            for tile in range(tile_count)
            for there, to in [target(lev, tile)]
        ]
        return lax.ppermute(array, ("lev", "tile"), pairs)

    def outward(lev, tile):
        return lev, (tile + (2 if tile % 2 else -2)) % tile_count

    def across(lev, tile):
        return lev, (tile + (1 if tile % 2 else -1)) % tile_count

    def other(lev, tile):
        return lev, tile ^ 1

    chips = lev_count // 2
    ops = lay_ops(column_ops, depth)

    def outspread(outs):
        return [
            send(outs[2 * a + b], lambda lev, tile: (lev ^ 2 * a, tile ^ b)) if a + b else outs[0]
            for a in range(chips)
            for b in range(2)
        ]

    def both_cores(blocks):
        return blocks + [send(block, lambda lev, tile: (lev ^ 1, tile)) for block in blocks]

    def mixed_back(chunk, blocks, earlier):
        mixed = mix(chunk, land_use, ops, blocks, earlier, chips)
        return [send(mixed[a], lambda lev, tile: (lev ^ 2 * a, tile)) if a else mixed[0] for a in range(chips)]

    first, second = CHUNKS
    keep_a, away_a, near_a, far_a = prep(fields[:, first[0] : first[-1] + 1])
    recv_a = send(away_a, other)
    before_a = send(far_a, across)
    after_a = send(near_a, outward)
    keep_b, away_b, near_b, far_b = prep(fields[:, second[0] : second[-1] + 1])
    recv_a, after_a, away_b, near_b, far_b = lax.optimization_barrier((recv_a, after_a, away_b, near_b, far_b))
    recv_b = send(away_b, other)
    before_b = send(far_b, across)
    after_b = send(near_b, outward)
    outs_a = advect((before_a, keep_a, recv_a, after_a), None, chips)
    faces, outs_a = outs_a[:9], outs_a[9:]
    blocks_a = outspread(outs_a)
    outs_b = advect((before_b, keep_b, recv_b, after_b), faces, chips)
    blocks_b = outspread(outs_b)
    blocks_a = later(blocks_a, outs_b[0], ops)
    back_a = mixed_back(first, both_cores(blocks_a), outs_b[0])
    blocks_b = later(blocks_b, back_a[0])
    back_b = mixed_back(second, both_cores(blocks_b), back_a[0])
    held = final(first, back_a, None, fields.shape, 10**9)
    return final(second, back_b, held, fields.shape, 1)


def solution(mesh):
    in_specs = (P("lev", None, "tile", None), P("tile", None), P())
    out_specs = P("lev", None, "tile", None)
    return jax.shard_map(
        per_device, mesh=mesh, in_specs=in_specs, out_specs=out_specs, check_vma=False
    )
```

```python
import functools

import jax
import jax.numpy as jnp
from jax import lax
from jax.experimental import pallas as pl
from jax.experimental.pallas import tpu as pltpu
from jax.sharding import PartitionSpec as P

COURANT = 0.4
COEFS = (1.0 / 3.0, 0.5, 1.0)
CHUNKS = ((2, 3, 4), (0, 1))
HALO = 6
UNROLL = 4
VMEM = pl.BlockSpec(memory_space=pltpu.VMEM)
PARAMS = pltpu.CompilerParams(vmem_limit_bytes=14 * 2**20)
F32 = jnp.float32


def cost(flops, arrays):
    return pl.CostEstimate(flops=1, bytes_accessed=1, transcendentals=0)


def sds(*shape, dtype=F32):
    return jax.ShapeDtypeStruct(shape, dtype)


def prep_kernel(x_ref, keep_ref, send_ref, near_ref, far_ref):
    rows, _, half, _ = keep_ref.shape
    odd = lax.rem(lax.axis_index("tile"), 2)
    for n in range(keep_ref.shape[1]):
        kept = jnp.swapaxes(x_ref[pl.ds(odd * half, half), n], 0, 1)
        sent = jnp.swapaxes(x_ref[pl.ds((1 - odd) * half, half), n], 0, 1)
        for r in range(rows):
            turned = jnp.where(odd == 0, r, rows - 1 - r)
            keep_ref[turned, n] = kept[r]
            send_ref[rows - 1 - turned, n] = sent[r]
    for r in range(HALO):
        near_ref[r] = keep_ref[r]
        far_ref[r] = send_ref[rows - HALO + r]


def prep(part):
    depth, count, rows, ny = part.shape
    shape = sds(rows, count, depth // 2, ny)
    return pl.pallas_call(
        prep_kernel,
        out_shape=[shape, shape] + [sds(HALO, *shape.shape[1:])] * 2,
        in_specs=[VMEM],
        out_specs=[VMEM] * 4,
        compiler_params=PARAMS,
        cost_estimate=cost(shape.size * 2, [shape] * 4),
    )(part)


def ops_kernel(per, ops_ref, out_ref):
    total, cats, levels, _ = ops_ref.shape
    core = lax.rem(lax.axis_index("lev"), 2)
    line = lax.broadcasted_iota(jnp.int32, (levels, 3 * levels), 0)
    column = lax.broadcasted_iota(jnp.int32, (levels, 3 * levels), 1)
    outer = ((column == line) | (column == line + 2 * levels)).astype(jnp.bfloat16)
    middle = (column == line + levels).astype(jnp.bfloat16)
    for f in range(total):
        rows = []
        for cat in range(cats):
            for low in range(0, levels, 2 * per):
                rows.append(ops_ref[f, cat, pl.ds(pl.multiple_of(low + core * per, 8), per), :])
        rows = jnp.concatenate(rows, axis=0)
        high = rows.astype(jnp.bfloat16)
        low = (rows - high.astype(F32)).astype(jnp.bfloat16)
        spread = jnp.dot(high, outer, preferred_element_type=F32)
        spread = spread + jnp.dot(low, middle, preferred_element_type=F32)
        out_ref[f] = spread.astype(jnp.bfloat16)


def lay_ops(column_ops, per):
    total, cats, levels, _ = column_ops.shape
    out = sds(total, cats * levels // 2, 3 * levels, dtype=jnp.bfloat16)
    return pl.pallas_call(
        functools.partial(ops_kernel, per),
        out_shape=out,
        in_specs=[VMEM],
        out_specs=VMEM,
        compiler_params=PARAMS,
        cost_estimate=cost(out.size, [out, column_ops]),
    )(column_ops)


def later_kernel(*refs):
    pass


def later(arrays, *others):
    count = len(arrays)
    return list(
        pl.pallas_call(
            later_kernel,
            out_shape=[sds(*array.shape) for array in arrays],
            in_specs=[VMEM] * count + [pl.BlockSpec(memory_space=pl.ANY)] * len(others),
            out_specs=[VMEM] * count,
            input_output_aliases={n: n for n in range(count)},
            compiler_params=PARAMS,
        )(*arrays, *others)
    )


def roll(a, shift):
    return pltpu.roll(a, shift % a.shape[1], 1)


def in_groups(first, end, rows, state):
    if UNROLL is None:
        return rows(first, end - first, state)

    def body(step, state):
        return rows(first + step * UNROLL, UNROLL, state)

    return lax.fori_loop(0, (end - first) // UNROLL, body, state)


def stage_rows(first, last, base, off_base, old, off_old, new, off_new, faces, fields, scales):
    ux, vr, vl = faces

    def wind(i):
        if scales is not None:
            ux[i - first + 1] = (old[off_old + i, 0] + old[off_old + i + 1, 0]) * scales[0]
        return ux[i - first + 1]

    def face(i, n, u):
        near = old[off_old + i, n] + old[off_old + i + 1, n]
        far = old[off_old + i - 1, n] + old[off_old + i + 2, n]
        return u * (7.0 * near - far)

    def rows(low, count, flux):
        flux = list(flux)
        for more in range(count):
            i = low + more
            u = wind(i)
            for n in range(fields) if scales is None else (1, 0, *range(2, fields)):
                s = old[off_old + i, n]
                l1, l2, r1, r2 = roll(s, 1), roll(s, 2), roll(s, -1), roll(s, -2)
                left, right = s + l1, s + r1
                if scales is not None and n == 1:
                    vr[i - first] = right * scales[1]
                    vl[i - first] = left * scales[1]
                wide = vr[i - first] * (7.0 * right - (l1 + r2)) - vl[i - first] * (7.0 * left - (l2 + r1))
                here = face(i, n, u)
                new[off_new + i, n] = base[off_base + i, n] + ((here - flux[n]) + wide)
                flux[n] = here
        return tuple(flux)

    u = wind(first - 1)
    in_groups(first, last + 1, rows, tuple(face(first - 1, n, u) for n in range(fields)))


def gather_rows(parts, ext):
    at = 0
    for part in parts:
        for i in range(part.shape[0]):
            ext[at + i] = part[i]
        at += part.shape[0]


def scatter_blocks(adv, outs, chips, own):
    place = lax.axis_index("lev") // 2
    for a in range(chips):
        there = place ^ a
        for q in range(own):
            outs[2 * a][q] = adv[there * own + q]
            outs[2 * a + 1][q] = adv[2 * chips * own - 1 - there * own - q]


def advect_kernel(chips, winds, before, keep, recv, after, *refs):
    rows = 2 * keep.shape[0]
    own = keep.shape[0] // chips
    faces, outs = refs[:9], refs[9 : 9 + 2 * chips]
    ext, s1, s2, adv = refs[9 + 2 * chips :]
    gather_rows((before, keep, recv, after), ext)
    sign = jnp.where(lax.rem(lax.axis_index("tile"), 2) == 0, 1.0, -1.0).astype(F32)
    states = ((ext, HALO), (s1, HALO - 2), (s2, HALO - 4), (adv, 0))
    for k, coef in enumerate(COEFS):
        reach = HALO - 2 * (k + 1)
        scale = -COURANT * coef / 24.0
        stage_rows(
            -reach, rows - 1 + reach, ext, HALO, *states[k], *states[k + 1],
            faces[3 * k : 3 * k + 3], keep.shape[1], (sign * scale, scale) if winds else None,
        )
    scatter_blocks(adv, outs, chips, own)


def advect(parts, faces, chips):
    keep = parts[1]
    tile_rows, fields, half, ny = keep.shape
    rows = 2 * tile_rows
    own = tile_rows // chips
    block = sds(own, fields, half, ny)
    sizes = [rows + 2 * (HALO - 2 * (k + 1)) for k in range(3)]
    scratch = [pltpu.VMEM((n, fields, half, ny), F32) for n in (rows + 2 * HALO, *sizes[:2], rows)]
    blocks = [block] * (2 * chips)
    outs, args = blocks, parts
    if faces is None:
        outs = [sds(n, half, ny) for size in sizes for n in (size + 1, size, size)] + blocks
    else:
        args = (*parts, *faces)
    return pl.pallas_call(
        functools.partial(advect_kernel, chips, faces is None),
        out_shape=outs,
        in_specs=[VMEM] * len(args),
        out_specs=[VMEM] * len(outs),
        scratch_shapes=scratch,
        compiler_params=PARAMS,
        cost_estimate=cost(sum(sizes) * fields * half * ny * 30, args),
    )(*args)


def mix_kernel(chips, chunk, use_ref, ops_ref, *refs):
    blocks, outs = refs[: 4 * chips], refs[4 * chips + 1 : 5 * chips + 1]
    data, result = refs[5 * chips + 1 :]
    own, _, half, ny = blocks[0].shape
    levels, per = data.shape[0], 2 * half
    kept = chips * per
    cats = ops_ref.shape[1] // kept
    lev = lax.axis_index("lev")
    place, core = lev // 2, lax.rem(lev, 2)
    odd = lax.rem(lax.axis_index("tile"), 2)
    use = []
    for q in range(own):
        row = place * own + q
        row = jnp.where(odd == 0, row, use_ref.shape[0] - 1 - row)
        use.append(use_ref[pl.ds(row, 1), :])
    for n, f in enumerate(chunk):
        for c in range(2):
            for a in range(chips):
                for b in range(2):
                    source = 2 * (place ^ a) + (core ^ c)
                    at = pl.multiple_of(source * per + (odd ^ b) * half, 8)
                    for q in range(own):
                        data[pl.ds(at, half), q * ny : (q + 1) * ny] = blocks[2 * chips * c + 2 * a + b][q, n]
        for q in range(own):
            for col in range(0, ny, 256):
                cols = slice(q * ny + col, q * ny + col + 256)
                whole = data[:, cols]
                high = whole.astype(jnp.bfloat16)
                low = (whole - high.astype(F32)).astype(jnp.bfloat16)
                three = jnp.concatenate([high, high, low], axis=0)
                every = jnp.dot(ops_ref[f], three, preferred_element_type=F32)
                here = use[q][:, col : col + 256]
                mixed = every[:kept]
                for c in range(1, cats):
                    mixed = jnp.where(here == c, every[c * kept : (c + 1) * kept], mixed)
                result[:, cols] = mixed
        for a in range(chips):
            at = pl.multiple_of((place ^ a) * per, 8)
            for q in range(own):
                outs[a][q, n] = result[pl.ds(at, per), q * ny : (q + 1) * ny]


def mix(chunk, use, ops, blocks, earlier, chips):
    own, fields, half, ny = blocks[0].shape
    levels = ops.shape[2] // 3
    return pl.pallas_call(
        functools.partial(mix_kernel, chips, chunk),
        out_shape=[sds(own, fields, 2 * half, ny)] * chips,
        in_specs=[VMEM] * (2 + len(blocks)) + [pl.BlockSpec(memory_space=pl.ANY)],
        out_specs=[VMEM] * chips,
        scratch_shapes=[
            pltpu.VMEM((levels, own * ny), F32),
            pltpu.VMEM((levels // 2, own * ny), F32),
        ],
        compiler_params=PARAMS,
        cost_estimate=cost(2 * fields * ops.shape[1] * ops.shape[2] * own * ny, blocks),
    )(use, ops, *blocks, earlier)


def final_kernel(chips, chunk, *refs):
    blocks, (out, turn, done, sem) = refs[:chips], refs[-4:]
    place = lax.axis_index("lev") // 2
    odd = lax.rem(lax.axis_index("tile"), 2)
    copies = []
    for n, f in enumerate(chunk):
        for a in range(chips):
            own = blocks[a].shape[0]
            for q in range(own):
                row = (place ^ a) * own + q
                row = jnp.where(odd == 0, row, own * chips - 1 - row)
                turn[row] = blocks[a][q, n]
        for low in range(0, out.shape[0], 8):
            done[n, low : low + 8] = jnp.swapaxes(turn[:, low : low + 8], 0, 1)
        copies.append(pltpu.make_async_copy(done.at[n], out.at[:, f], sem.at[n]))
        copies[-1].start()
    for copy in copies:
        copy.wait()


def final(chunk, blocks, held, shape, size):
    depth, _, rows, ny = shape
    whole = [] if held is None else [held]
    return pl.pallas_call(
        functools.partial(final_kernel, len(blocks), chunk),
        out_shape=sds(*shape),
        in_specs=[VMEM] * len(blocks) + [pl.BlockSpec(memory_space=pl.ANY)] * len(whole),
        out_specs=pl.BlockSpec(memory_space=pl.ANY),
        input_output_aliases={len(blocks): 0} if whole else {},
        scratch_shapes=[
            pltpu.VMEM((rows, depth, ny), F32),
            pltpu.VMEM((len(chunk), depth, rows, ny), F32),
            pltpu.SemaphoreType.DMA((len(chunk),)),
        ],
        compiler_params=PARAMS,
        cost_estimate=pl.CostEstimate(flops=size, bytes_accessed=1, transcendentals=0),
    )(*blocks, *whole)


def per_device(fields, land_use, column_ops):
    lev_count, tile_count = lax.axis_size("lev"), lax.axis_size("tile")
    depth, total, rows, ny = fields.shape

    def send(array, target):
        pairs = [
            (lev * tile_count + tile, there * tile_count + to)
            for lev in range(lev_count)
            for tile in range(tile_count)
            for there, to in [target(lev, tile)]
        ]
        return lax.ppermute(array, ("lev", "tile"), pairs)

    def outward(lev, tile):
        return lev, (tile + (2 if tile % 2 else -2)) % tile_count

    def across(lev, tile):
        return lev, (tile + (1 if tile % 2 else -1)) % tile_count

    def other(lev, tile):
        return lev, tile ^ 1

    chips = lev_count // 2
    ops = lay_ops(column_ops, depth)

    def outspread(outs):
        return [
            send(outs[2 * a + b], lambda lev, tile: (lev ^ 2 * a, tile ^ b)) if a + b else outs[0]
            for a in range(chips)
            for b in range(2)
        ]

    def both_cores(blocks):
        return blocks + [send(block, lambda lev, tile: (lev ^ 1, tile)) for block in blocks]

    def mixed_back(chunk, blocks, earlier):
        mixed = mix(chunk, land_use, ops, blocks, earlier, chips)
        return [send(mixed[a], lambda lev, tile: (lev ^ 2 * a, tile)) if a else mixed[0] for a in range(chips)]

    first, second = CHUNKS
    keep_a, away_a, near_a, far_a = prep(fields[:, first[0] : first[-1] + 1])
    recv_a = send(away_a, other)
    before_a = send(far_a, across)
    after_a = send(near_a, outward)
    keep_b, away_b, near_b, far_b = prep(fields[:, second[0] : second[-1] + 1])
    before_a, away_b, near_b, far_b = lax.optimization_barrier((before_a, away_b, near_b, far_b))
    recv_b = send(away_b, other)
    before_b = send(far_b, across)
    after_b = send(near_b, outward)
    outs_a = advect((before_a, keep_a, recv_a, after_a), None, chips)
    faces, outs_a = outs_a[:9], outs_a[9:]
    blocks_a = outspread(outs_a)
    outs_b = advect((before_b, keep_b, recv_b, after_b), faces, chips)
    blocks_b = outspread(outs_b)
    blocks_a = later(blocks_a, *blocks_b[1:], ops)
    back_a = mixed_back(first, both_cores(blocks_a), outs_b[0])
    blocks_b = later(blocks_b, back_a[0])
    back_b = mixed_back(second, both_cores(blocks_b), back_a[0])
    held = final(first, back_a, None, fields.shape, 10**9)
    return final(second, back_b, held, fields.shape, 1)


def solution(mesh):
    in_specs = (P("lev", None, "tile", None), P("tile", None), P())
    out_specs = P("lev", None, "tile", None)
    return jax.shard_map(
        per_device, mesh=mesh, in_specs=in_specs, out_specs=out_specs, check_vma=False
    )
```
